256 devices in a mesh: ctx: 32 (over y, x, core), head: 8 (over z).
Axes of the slice: x: 4, y: 4, z: 8, core: 2. Of those that a mesh axis runs over, the one named last changes fastest.
Arguments:
- queries: bfloat16 [4096, 8192], P('ctx', 'head'), may hold values from -90 to 90
- keys: bfloat16 [4096, 1024], P('ctx', 'head'), may hold values from -4 to 4
- values: bfloat16 [4096, 1024], P('ctx', 'head'), may hold values from -5 to 5
- out_grad: bfloat16 [4096, 8192], P('ctx', 'head'), may hold values from -5 to 5
- block_order: int32 [64], replicated, may hold values from 0 to 63, each once
Outputs:
- grads: bfloat16 [4096, 10240], P(('ctx', 'head'))
The draws below stay inside these ranges and needn't reach their ends.
All inputs are finite; a program needn't handle non-finite values.
Results may differ from the reference program's by a relative error of at most 0.006.
Values may be sent and summed in bfloat16 or wider, within the bound.
No kernel may reach another device: no remote copies, remote signals or barrier semaphores. Data moves between devices by JAX's collectives and lax.ppermute only.
A program may use at most 64 MiB of HBM per device.

```python
import jax
import jax.numpy as jnp
from jax import lax

HD = 128
KVH = 8
QGROUP = 8
QHEADS = 64
BLOCK = 64
SEQ = 4096
NBLOCKS = 64


def base_keys(key):
    return jnp.clip(jax.random.normal(key, (SEQ, KVH * HD), jnp.float32), -4.0, 4.0)


def draw_keys(key, part):
    base = base_keys(key)
    return base.astype(jnp.bfloat16)


def draw_queries(key, part):
    key = jax.random.fold_in(key, 5)
    drawn = jnp.clip(jax.random.normal(key, (SEQ, QHEADS * HD), jnp.float32), -4.0, 4.0)
    return drawn.astype(jnp.bfloat16)


def shard_levels(key, shape, cuts, low, top_value):
    def one(dim, shards_of):
        heights = jax.random.uniform(jax.random.fold_in(jax.random.fold_in(key, 6), dim), (shards_of,), jnp.float32, low / len(cuts), top_value / len(cuts))
        return jnp.repeat(jnp.exp(heights), shape[dim] // shards_of).reshape((-1,) + (1,) * (len(shape) - dim - 1))

    loudness = one(*cuts[0])
    for cut in cuts[1:]:
        loudness = loudness * one(*cut)
    return loudness


def scatter_about(rng, extent, scale, most, pieces=(), kind=jnp.bfloat16):
    array = jax.random.normal(rng, extent, jnp.float32) * scale
    if len(pieces) > 0:
        array = shard_levels(rng, extent, pieces, -0.22, 0.18) * array
    return jnp.clip(array, min=-most, max=most).astype(kind)


def setup_inputs(seed: int = 0) -> dict:
    arg_keys = jax.random.split(jax.random.key(seed), 6)
    queries = draw_queries(jax.random.fold_in(arg_keys[5], 71), 0)
    keys = draw_keys(jax.random.fold_in(arg_keys[5], 71), 0)
    values = scatter_about(arg_keys[2], (SEQ, KVH * HD), 1.0, 5.0, ((0, 32), (1, 8)))
    out_grad = scatter_about(arg_keys[3], (SEQ, QHEADS * HD), 1.0, 5.0, ((0, 32), (1, 8)))
    block_order = jax.random.permutation(arg_keys[4], NBLOCKS).astype(jnp.int32)
    return dict(queries=queries, keys=keys, values=values, out_grad=out_grad, block_order=block_order)


NEG = -1e30


def one_head(query_head, key_head, value_head, grad_head, allowed):
    score_scale = HD ** -0.5
    score = jnp.dot(query_head, key_head.T, preferred_element_type=jnp.float32) * score_scale
    score = jnp.where(allowed, score, NEG)
    row_top = jnp.max(score, axis=1, keepdims=True)
    row_total = jnp.sum(jnp.exp(score - row_top), axis=1, keepdims=True)
    log_total = row_top + jnp.log(row_total)
    attn_probs = jnp.exp(score - log_total)
    grad_probs = jnp.dot(grad_head, value_head.T, preferred_element_type=jnp.float32)
    row_delta = jnp.sum(attn_probs * grad_probs, axis=1, keepdims=True)
    grad_score = (attn_probs * (grad_probs - row_delta) * score_scale).astype(jnp.bfloat16)
    probs_low = attn_probs.astype(jnp.bfloat16)
    grad_query = jnp.dot(grad_score, key_head, preferred_element_type=jnp.float32)
    grad_key = jnp.dot(grad_score.T, query_head, preferred_element_type=jnp.float32)
    grad_value = jnp.dot(probs_low.T, grad_head, preferred_element_type=jnp.float32)
    return grad_query, grad_key, grad_value


def reference(queries, keys, values, out_grad, block_order):
    rows = jnp.arange(SEQ, dtype=jnp.int32)
    positions = block_order[rows // BLOCK] * BLOCK + rows % BLOCK
    allowed = positions[None, :] <= positions[:, None]
    query_heads = queries.reshape(SEQ, QHEADS, HD).transpose(1, 0, 2)
    grad_heads = out_grad.reshape(SEQ, QHEADS, HD).transpose(1, 0, 2)
    key_heads = keys.reshape(SEQ, KVH, HD).transpose(1, 0, 2)
    value_heads = values.reshape(SEQ, KVH, HD).transpose(1, 0, 2)

    def per_head(index):
        group = index // QGROUP
        return one_head(query_heads[index], key_heads[group], value_heads[group], grad_heads[index], allowed)

    grad_query, grad_key, grad_value = lax.map(per_head, jnp.arange(QHEADS, dtype=jnp.int32))
    grad_key = jnp.sum(grad_key.reshape(KVH, QGROUP, SEQ, HD), axis=1)
    grad_value = jnp.sum(grad_value.reshape(KVH, QGROUP, SEQ, HD), axis=1)
    query_cols = grad_query.transpose(1, 0, 2).reshape(SEQ, QHEADS * HD)
    key_cols = grad_key.transpose(1, 0, 2).reshape(SEQ, KVH * HD)
    value_cols = grad_value.transpose(1, 0, 2).reshape(SEQ, KVH * HD)
    return jnp.concatenate([query_cols, key_cols, value_cols], axis=1).astype(jnp.bfloat16)
```

```python
import functools

import jax
import jax.numpy as jnp
from jax import lax
from jax.experimental import pallas as pl
from jax.experimental.pallas import tpu as pltpu
from jax.sharding import Mesh, PartitionSpec as P

HD = 128
QGROUP = 8
BLOCK = 64
NBLOCKS = 64
TOK = 128
CHIPS = 16
SEQ = 4096
TILE = 256
TILES = SEQ // TILE
ROWS = QGROUP * BLOCK
NEG = -1e30
SCALE = HD**-0.5
LOG2E = 1.4426950408889634


def mm(a, b):
    return jnp.dot(a, b, preferred_element_type=jnp.float32)


def fold(x, op):
    return op(x.reshape(x.shape[0] // 8, 8, x.shape[1]), axis=0)


def attention_kernel(
    order, place, q, g, own, other, dq, keep, send, ks, vs, kt, dk, dv, s_all, dp_all, qr, gr, qt, gt
):
    ctx = place[0]
    core = lax.rem(ctx, 2)
    chip_slots = [(i // 2) * 4 + i % 2 for i in range(2 * CHIPS)]

    def sorted_rows(i, half):
        start = order[chip_slots[i] + half * 2] * BLOCK
        return pl.ds(pl.multiple_of(start, BLOCK), BLOCK)

    for i in range(2 * CHIPS):
        rows = slice(i * BLOCK, (i + 1) * BLOCK)
        for src, half in ((own, core), (other, 1 - core)):
            dst = sorted_rows(i, half)
            ks[dst, :] = src[rows, :HD]
            vs[dst, :] = src[rows, HD:]

    def prepare(t, carry):
        rows = pl.ds(pl.multiple_of(t * TILE, TILE), TILE)
        kt[t] = ks[rows, :].T
        dk[t] = jnp.zeros((TILE, HD), jnp.float32)
        dv[t] = jnp.zeros((TILE, HD), jnp.float32)
        return carry

    lax.fori_loop(0, TILES, prepare, 0)

    for u in range(TOK // BLOCK):
        block = order[ctx * 2 + u]
        last = block // (TILE // BLOCK)
        for h in range(QGROUP):
            part = (slice(u * BLOCK, (u + 1) * BLOCK), slice(h * HD, (h + 1) * HD))
            qr[h * BLOCK : (h + 1) * BLOCK, :] = q[part]
            gr[h * BLOCK : (h + 1) * BLOCK, :] = g[part]
        qt[...] = qr[...].T
        gt[...] = gr[...].T

        def score(t):
            rows = pl.ds(pl.multiple_of(t * TILE, TILE), TILE)
            return mm(ks[rows, :], qt[...])

        def top_step(t, top):
            s = score(t)
            s_all[t] = s
            return jnp.maximum(top, fold(s, jnp.max))

        top = lax.fori_loop(0, last, top_step, jnp.full((8, ROWS), NEG, jnp.float32))
        s = score(last)
        key_pos = last * TILE + lax.broadcasted_iota(jnp.int32, s.shape, 0)
        row_pos = block * BLOCK + lax.rem(lax.broadcasted_iota(jnp.int32, s.shape, 1), BLOCK)
        s = jnp.where(key_pos <= row_pos, s, NEG)
        s_all[last] = s
        top = jnp.max(jnp.maximum(top, fold(s, jnp.max)), axis=0, keepdims=True)

        def sum_step(t, carry):
            total, delta = carry
            rows = pl.ds(pl.multiple_of(t * TILE, TILE), TILE)
            dp = mm(vs[rows, :], gt[...])
            p = jnp.exp2((s_all[t] - top) * (SCALE * LOG2E))
            s_all[t] = p
            dp_all[t] = dp
            return (total + fold(p, jnp.sum), delta + fold(p * dp, jnp.sum))

        zero = jnp.zeros((8, ROWS), jnp.float32)
        total, delta = lax.fori_loop(0, last + 1, sum_step, (zero, zero))
        inv = 1.0 / jnp.sum(total, axis=0, keepdims=True)
        delta = jnp.sum(delta, axis=0, keepdims=True) * inv

        def grad_step(t, dqt):
            p = s_all[t] * inv
            ds = (p * (dp_all[t] - delta) * SCALE).astype(jnp.bfloat16)
            dv[t] += mm(p.astype(jnp.bfloat16), gr[...])
            dk[t] += mm(ds, qr[...])
            return dqt + mm(kt[t], ds)

        dqt = lax.fori_loop(0, last + 1, grad_step, jnp.zeros((HD, ROWS), jnp.float32))
        out = dqt.T.astype(jnp.bfloat16)
        for h in range(QGROUP):
            part = (slice(u * BLOCK, (u + 1) * BLOCK), slice(h * HD, (h + 1) * HD))
            dq[part] = out[h * BLOCK : (h + 1) * BLOCK, :]

    for i in range(2 * CHIPS):
        rows = slice(i * BLOCK, (i + 1) * BLOCK)
        for dst, half in ((keep, core), (send, 1 - core)):
            block = order[chip_slots[i] + half * 2]
            tile = block // (TILE // BLOCK)
            src = pl.ds(pl.multiple_of(lax.rem(block, TILE // BLOCK) * BLOCK, BLOCK), BLOCK)
            dst[rows, :HD] = dk[tile, src, :].astype(jnp.bfloat16)
            dst[rows, HD:] = dv[tile, src, :].astype(jnp.bfloat16)


def attention(order, place, q, g, own, other):
    smem = pl.BlockSpec(memory_space=pltpu.SMEM)
    vmem = pl.BlockSpec(memory_space=pltpu.VMEM)
    half = CHIPS * TOK
    bf16, f32 = jnp.bfloat16, jnp.float32
    return pl.pallas_call(
        attention_kernel,
        out_shape=(
            jax.ShapeDtypeStruct((TOK, QGROUP * HD), bf16),
            jax.ShapeDtypeStruct((half, 2 * HD), bf16),
            jax.ShapeDtypeStruct((half, 2 * HD), bf16),
        ),
        in_specs=[smem, smem, vmem, vmem, vmem, vmem],
        out_specs=(vmem, vmem, vmem),
        scratch_shapes=[
            pltpu.VMEM((SEQ, HD), bf16),
            pltpu.VMEM((SEQ, HD), bf16),
            pltpu.VMEM((TILES, HD, TILE), bf16),
            pltpu.VMEM((TILES, TILE, HD), f32),
            pltpu.VMEM((TILES, TILE, HD), f32),
            pltpu.VMEM((TILES, TILE, ROWS), f32),
            pltpu.VMEM((TILES, TILE, ROWS), f32),
            pltpu.VMEM((ROWS, HD), bf16),
            pltpu.VMEM((ROWS, HD), bf16),
            pltpu.VMEM((HD, ROWS), bf16),
            pltpu.VMEM((HD, ROWS), bf16),
        ],
        compiler_params=pltpu.CompilerParams(vmem_limit_bytes=48 * 1024 * 1024),
        cost_estimate=pl.CostEstimate(
            flops=10 * TOK * QGROUP * SEQ * HD, bytes_accessed=6 * 1024 * 1024, transcendentals=TOK * QGROUP * SEQ
        ),
        name="attention",
    )(order, place, q, g, own, other)


def shards(queries, keys, values, out_grad, block_order):
    swap = [(0, 1), (1, 0)]
    plane = ("y", "x")
    kv = jnp.concatenate([keys, values], axis=1)
    spread = jnp.broadcast_to(kv[None], (CHIPS,) + kv.shape)
    own = lax.all_to_all(spread, plane, 0, 0, tiled=True).reshape(CHIPS * TOK, 2 * HD)
    other = lax.ppermute(own, "core", swap)
    place = lax.axis_index(("y", "x", "core")).astype(jnp.int32).reshape(1)
    dq, keep, send = attention(block_order, place, queries, out_grad, own, other)
    came = lax.ppermute(send, "core", swap)
    pair = (keep.astype(jnp.float32) + came.astype(jnp.float32)).astype(jnp.bfloat16)
    parts = lax.all_to_all(pair.reshape(CHIPS, TOK, 2 * HD), plane, 0, 0, tiled=True)
    dkv = jnp.sum(parts.astype(jnp.float32), axis=0).astype(jnp.bfloat16)
    mine = jnp.concatenate([dq, dkv], axis=1).reshape(8, TOK // 8, 10 * HD)
    got = lax.all_to_all(mine, "head", 0, 0, tiled=True).transpose(1, 0, 2)
    cols = [got[:, :, : 8 * HD], got[:, :, 8 * HD : 9 * HD], got[:, :, 9 * HD :]]
    return jnp.concatenate([c.reshape(TOK // 8, -1) for c in cols], axis=1)


def solution(mesh):
    split = Mesh(mesh.devices.reshape(4, 4, 2, 8), ("y", "x", "core", "head"))
    ctx = ("y", "x", "core")
    rows = P(ctx, "head")
    return jax.shard_map(
        shards,
        mesh=split,
        in_specs=(rows, rows, rows, rows, P()),
        out_specs=P(ctx + ("head",), None),
        check_vma=False,
    )
```

```python
import jax
import jax.numpy as jnp
from jax import lax
from jax.experimental import pallas as pl
from jax.experimental.pallas import tpu as pltpu
from jax.sharding import Mesh, PartitionSpec as P

HD = 128
QGROUP = 8
BLOCK = 64
TOK = 128
CHIPS = 16
HALF = CHIPS * TOK
OWN_BLOCKS = HALF // BLOCK
UNITS = 4
TILE = 256
STEP = 1024
ROWS = QGROUP * BLOCK
NEG = -1e30
SCALE = HD**-0.5
LOG2E = 1.4426950408889634
BF16 = jnp.bfloat16
F32 = jnp.float32


def mm(a, b):
    return jnp.dot(a, b, preferred_element_type=F32)


def fold(x, op):
    return op(x.reshape(x.shape[0] // 8, 8, x.shape[1]), axis=0)


def step_rows(i):
    return pl.ds(pl.multiple_of(i * STEP, STEP), STEP)


def block_rows(i):
    return pl.ds(pl.multiple_of(i * BLOCK, BLOCK), BLOCK)


def unit_rows(u):
    return pl.ds(pl.multiple_of(u * ROWS, ROWS), ROWS)


def stats_kernel(
    order, place, q_own, q_other, g_own, g_other, kv,
    stats, p_all, dp_all, kt, qr, gr, rank, held,
    ks, vs, qt, gt, owner, upto,
):
    ctx = place[0]
    core = lax.rem(ctx, 2)

    def clear(p, carry):
        owner[p] = -1
        return carry

    lax.fori_loop(0, 2 * OWN_BLOCKS, clear, 0, unroll=True)
    for i in range(OWN_BLOCKS):
        owner[order[(i // 2) * 4 + core * 2 + i % 2]] = i

    def count(p, seen):
        i = owner[p]
        mine = i >= 0

        @pl.when(mine)
        def _():
            rank[i] = seen

        seen = seen + mine.astype(jnp.int32)
        upto[p] = seen
        return seen

    lax.fori_loop(0, 2 * OWN_BLOCKS, count, 0)

    for i in range(OWN_BLOCKS):
        rows = slice(i * BLOCK, (i + 1) * BLOCK)
        dst = block_rows(rank[i])
        ks[dst, :] = kv[rows, :HD]
        vs[dst, :] = kv[rows, HD:]
    for j in range(HALF // TILE):
        kt[j] = ks[j * TILE : (j + 1) * TILE, :].T
    for u in range(UNITS):
        q, g = ((q_own, g_own), (q_other, g_other))[u // 2]
        for h in range(QGROUP):
            part = (slice(u % 2 * BLOCK, (u % 2 + 1) * BLOCK), slice(h * HD, (h + 1) * HD))
            rows = slice(u * ROWS + h * BLOCK, u * ROWS + (h + 1) * BLOCK)
            qr[rows, :] = q[part]
            gr[rows, :] = g[part]

    def unit(u, carry):
        slot = (ctx + (u // 2) * (1 - 2 * core)) * 2 + lax.rem(u, 2)
        block = order[slot]
        seen = upto[block]
        held[u] = seen
        steps = (seen * BLOCK + STEP - 1) // STEP
        diagonal = owner[block] >= 0
        lane = lax.rem(lax.broadcasted_iota(jnp.int32, (1, ROWS), 1), BLOCK)
        limit = (seen - 1) * BLOCK + jnp.where(diagonal, lane, BLOCK - 1)
        qt[...] = qr[unit_rows(u), :].T
        gt[...] = gr[unit_rows(u), :].T

        def top_step(i, top):
            s = mm(ks[step_rows(i), :], qt[...])
            key = lax.broadcasted_iota(jnp.int32, s.shape, 0)
            s = jnp.where(key <= limit - i * STEP, s, NEG)
            p_all[u, step_rows(i), :] = s
            return jnp.maximum(top, fold(s, jnp.max))

        top = lax.fori_loop(0, steps, top_step, jnp.full((8, ROWS), NEG, F32))
        top = jnp.max(top, axis=0, keepdims=True)

        def sum_step(i, carry):
            total, delta = carry
            rows = step_rows(i)
            dp = mm(vs[rows, :], gt[...])
            p = jnp.exp2((p_all[u, rows, :] - top) * (SCALE * LOG2E))
            p_all[u, rows, :] = p
            dp_all[u, rows, :] = dp
            return (total + fold(p, jnp.sum), delta + fold(p * dp, jnp.sum))

        zero = jnp.zeros((8, ROWS), F32)
        total, delta = lax.fori_loop(0, steps, sum_step, (zero, zero))
        stats[u, 0:1, :] = top
        stats[u, 1:2, :] = jnp.sum(total, axis=0, keepdims=True)
        stats[u, 2:3, :] = jnp.sum(delta, axis=0, keepdims=True)
        stats[u, 3:8, :] = jnp.zeros((5, ROWS), F32)
        return carry

    lax.fori_loop(0, UNITS, unit, 0)


def grads_kernel(
    rank, held, stats, came, p_all, dp_all, kt, qr, gr,
    dq_own, dq_other, dkv,
    dk, dv, dqt,
):
    dk[...] = jnp.zeros((HALF, HD), F32)
    dv[...] = jnp.zeros((HALF, HD), F32)
    dqt[...] = jnp.zeros((UNITS, HD, ROWS), F32)

    def unit(u, carry):
        other = lax.rem(u + 2, UNITS)
        steps = (held[u] * BLOCK + STEP - 1) // STEP
        top, total, delta = (stats[u, k : k + 1, :] for k in range(3))
        top2, total2, delta2 = (came[other, k : k + 1, :] for k in range(3))
        both = jnp.maximum(top, top2)
        w = jnp.exp2((top - both) * (SCALE * LOG2E))
        w2 = jnp.exp2((top2 - both) * (SCALE * LOG2E))
        inv = 1.0 / (total * w + total2 * w2)
        delta = (delta * w + delta2 * w2) * inv
        w = w * inv

        def grad_step(i, carry):
            rows = step_rows(i)
            p = p_all[u, rows, :] * w
            ds = (p * (dp_all[u, rows, :] - delta) * SCALE).astype(BF16)
            dv[rows, :] += mm(p.astype(BF16), gr[unit_rows(u), :])
            dk[rows, :] += mm(ds, qr[unit_rows(u), :])
            part = mm(kt[i * (STEP // TILE)], ds[:TILE])
            for j in range(1, STEP // TILE):
                part += mm(kt[i * (STEP // TILE) + j], ds[j * TILE : (j + 1) * TILE])
            dqt[u] += part
            return carry

        lax.fori_loop(0, steps, grad_step, 0)
        return carry

    lax.fori_loop(0, UNITS, unit, 0)
    for u in range(UNITS):
        dq = (dq_own, dq_other)[u // 2]
        out = dqt[u].T
        for h in range(QGROUP):
            part = (slice(u % 2 * BLOCK, (u % 2 + 1) * BLOCK), slice(h * HD, (h + 1) * HD))
            dq[part] = out[h * BLOCK : (h + 1) * BLOCK, :]
    for i in range(OWN_BLOCKS):
        rows = slice(i * BLOCK, (i + 1) * BLOCK)
        src = block_rows(rank[i])
        dkv[rows, :HD] = dk[src, :].astype(BF16)
        dkv[rows, HD:] = dv[src, :].astype(BF16)


def attention(order, place, q_own, q_other, g_own, g_other, kv, swap):
    smem = pl.BlockSpec(memory_space=pltpu.SMEM)
    vmem = pl.BlockSpec(memory_space=pltpu.VMEM)
    shape = jax.ShapeDtypeStruct
    params = pltpu.CompilerParams(vmem_limit_bytes=10 * 1024 * 1024)
    pairs = UNITS * ROWS * HALF
    stats, p_all, dp_all, kt, qr, gr, rank, held = pl.pallas_call(
        stats_kernel,
        out_shape=(
            shape((UNITS, 8, ROWS), F32),
            shape((UNITS, HALF, ROWS), F32),
            shape((UNITS, HALF, ROWS), F32),
            shape((HALF // TILE, HD, TILE), BF16),
            shape((UNITS * ROWS, HD), BF16),
            shape((UNITS * ROWS, HD), BF16),
            shape((OWN_BLOCKS,), jnp.int32),
            shape((UNITS,), jnp.int32),
        ),
        in_specs=[smem, smem] + [vmem] * 5,
        out_specs=(vmem,) * 6 + (smem, smem),
        scratch_shapes=[
            pltpu.VMEM((HALF, HD), BF16),
            pltpu.VMEM((HALF, HD), BF16),
            pltpu.VMEM((HD, ROWS), BF16),
            pltpu.VMEM((HD, ROWS), BF16),
            pltpu.SMEM((2 * OWN_BLOCKS,), jnp.int32),
            pltpu.SMEM((2 * OWN_BLOCKS,), jnp.int32),
        ],
        compiler_params=params,
        cost_estimate=pl.CostEstimate(flops=4 * pairs * HD, bytes_accessed=4 * 2**20, transcendentals=pairs),
        name="stats",
    )(order, place, q_own, q_other, g_own, g_other, kv)
    came = swap(stats)
    return pl.pallas_call(
        grads_kernel,
        out_shape=(
            shape((TOK, QGROUP * HD), F32),
            shape((TOK, QGROUP * HD), F32),
            shape((HALF, 2 * HD), BF16),
        ),
        in_specs=[smem, smem] + [vmem] * 7,
        out_specs=(vmem,) * 3,
        scratch_shapes=[
            pltpu.VMEM((HALF, HD), F32),
            pltpu.VMEM((HALF, HD), F32),
            pltpu.VMEM((UNITS, HD, ROWS), F32),
        ],
        compiler_params=params,
        cost_estimate=pl.CostEstimate(flops=6 * pairs * HD, bytes_accessed=4 * 2**20, transcendentals=0),
        name="grads",
    )(rank, held, stats, came, p_all, dp_all, kt, qr, gr)


def shards(queries, keys, values, out_grad, block_order):
    plane = ("y", "x")

    def swap(x):
        return lax.ppermute(x, "core", [(0, 1), (1, 0)])

    q_other, g_other = swap(queries), swap(out_grad)
    kv = jnp.concatenate([keys, values], axis=1)
    spread = jnp.broadcast_to(kv[None], (CHIPS,) + kv.shape)
    gathered = lax.all_to_all(spread, plane, 0, 0, tiled=True).reshape(HALF, 2 * HD)
    place = lax.axis_index(("y", "x", "core")).astype(jnp.int32).reshape(1)
    dq_own, dq_other, dkv = attention(
        block_order, place, queries, q_other, out_grad, g_other, gathered, swap
    )
    dq_came = swap(dq_other)
    parts = lax.all_to_all(dkv.reshape(CHIPS, TOK, 2 * HD), plane, 0, 0, tiled=True)
    dkv = jnp.sum(parts.astype(F32), axis=0).astype(BF16)
    dq = (dq_own + dq_came).astype(BF16)
    mine = jnp.concatenate([dq, dkv], axis=1).reshape(8, TOK // 8, 10 * HD)
    got = lax.all_to_all(mine, "head", 0, 0, tiled=True).transpose(1, 0, 2)
    cols = [got[:, :, : 8 * HD], got[:, :, 8 * HD : 9 * HD], got[:, :, 9 * HD :]]
    return jnp.concatenate([c.reshape(TOK // 8, -1) for c in cols], axis=1)


def solution(mesh):
    split = Mesh(mesh.devices.reshape(4, 4, 2, 8), ("y", "x", "core", "head"))
    ctx = ("y", "x", "core")
    rows = P(ctx, "head")
    return jax.shard_map(
        shards,
        mesh=split,
        in_specs=(rows, rows, rows, rows, P()),
        out_specs=P(ctx + ("head",), None),
        check_vma=False,
    )
```

```python
import jax
import jax.numpy as jnp
from jax import lax
from jax.experimental import pallas as pl
from jax.experimental.pallas import tpu as pltpu
from jax.sharding import Mesh, PartitionSpec as P

HD = 128
QGROUP = 8
BLOCK = 64
TOK = 128
CHIPS = 16
HALF = CHIPS * TOK
OWN_BLOCKS = HALF // BLOCK
UNITS = 4
STEP = 1024
SEEN = OWN_BLOCKS
DIAGONAL = SEEN + UNITS
VMEM_LIMIT = 10 * 2**20
ROWS = QGROUP * BLOCK
NEG = -1e30
SCALE = HD**-0.5
LOG2E = 1.4426950408889634
BF16 = jnp.bfloat16
F32 = jnp.float32


def mm(a, b):
    return jnp.dot(a, b, preferred_element_type=F32)


def mm_t(a, b):
    return lax.dot_general(a, b, (((1,), (1,)), ((), ())), preferred_element_type=F32)


def fold(x, op):
    return op(x.reshape(x.shape[0] // 8, 8, x.shape[1]), axis=0)


def step_rows(i):
    return pl.ds(pl.multiple_of(i * STEP, STEP), STEP)


def block_rows(i):
    return pl.ds(pl.multiple_of(i * BLOCK, BLOCK), BLOCK)


def prep_kernel(order, place, q_own, q_other, g_own, g_other, meta, rows_qg, owner, upto):
    ctx = place[0]
    core = lax.rem(ctx, 2)

    def clear(p, carry):
        owner[p] = -1
        return carry

    lax.fori_loop(0, 2 * OWN_BLOCKS, clear, 0, unroll=True)
    for i in range(OWN_BLOCKS):
        owner[order[(i // 2) * 4 + core * 2 + i % 2]] = i

    def count(p, seen):
        i = owner[p]
        mine = i >= 0

        @pl.when(mine)
        def _():
            meta[i] = seen

        seen = seen + mine.astype(jnp.int32)
        upto[p] = seen
        return seen

    lax.fori_loop(0, 2 * OWN_BLOCKS, count, 0)
    for u in range(UNITS):
        block = order[(ctx + (u // 2) * (1 - 2 * core)) * 2 + u % 2]
        meta[SEEN + u] = upto[block]
        meta[DIAGONAL + u] = (owner[block] >= 0).astype(jnp.int32)
        q, g = ((q_own, g_own), (q_other, g_other))[u // 2]
        for h in range(QGROUP):
            part = (slice(u % 2 * BLOCK, (u % 2 + 1) * BLOCK), slice(h * HD, (h + 1) * HD))
            rows = slice(h * BLOCK, (h + 1) * BLOCK)
            rows_qg[0, u, rows, :] = q[part]
            rows_qg[1, u, rows, :] = g[part]


def steps_of(meta, u):
    return (meta[SEEN + u] * BLOCK + STEP - 1) // STEP


def stats_kernel(meta, kv, rows_qg, stats, p_all, dp_all, ks, vs):
    for i in range(OWN_BLOCKS):
        rows = slice(i * BLOCK, (i + 1) * BLOCK)
        dst = block_rows(meta[i])
        ks[dst, :] = kv[rows, :HD]
        vs[dst, :] = kv[rows, HD:]

    def unit(u, carry):
        steps = steps_of(meta, u)
        lane = lax.rem(lax.broadcasted_iota(jnp.int32, (1, ROWS), 1), BLOCK)
        limit = (meta[SEEN + u] - 1) * BLOCK + jnp.where(meta[DIAGONAL + u] > 0, lane, BLOCK - 1)

        def top_step(i, top):
            s = mm_t(ks[step_rows(i), :], rows_qg[0, u])
            key = lax.broadcasted_iota(jnp.int32, s.shape, 0)
            s = jnp.where(key <= limit - i * STEP, s, NEG)
            p_all[u, step_rows(i), :] = s
            return jnp.maximum(top, fold(s, jnp.max))

        top = lax.fori_loop(0, steps, top_step, jnp.full((8, ROWS), NEG, F32))
        top = jnp.max(top, axis=0, keepdims=True)

        def sum_step(i, carry):
            total, delta = carry
            rows = step_rows(i)
            dp = mm_t(vs[rows, :], rows_qg[1, u])
            p = jnp.exp2((p_all[u, rows, :] - top) * (SCALE * LOG2E))
            p_all[u, rows, :] = p
            dp_all[u, rows, :] = dp
            return (total + fold(p, jnp.sum), delta + fold(p * dp, jnp.sum))

        zero = jnp.zeros((8, ROWS), F32)
        total, delta = lax.fori_loop(0, steps, sum_step, (zero, zero))
        stats[u, 0:1, :] = top
        stats[u, 1:2, :] = jnp.sum(total, axis=0, keepdims=True)
        stats[u, 2:3, :] = jnp.sum(delta, axis=0, keepdims=True)
        stats[u, 3:8, :] = jnp.zeros((5, ROWS), F32)
        return carry

    lax.fori_loop(0, UNITS, unit, 0)


def merge(stats, came, u):
    other = lax.rem(u + 2, UNITS)
    top, total, delta = (stats[u, k : k + 1, :] for k in range(3))
    top2, total2, delta2 = (came[other, k : k + 1, :] for k in range(3))
    both = jnp.maximum(top, top2)
    w = jnp.exp2((top - both) * (SCALE * LOG2E))
    w2 = jnp.exp2((top2 - both) * (SCALE * LOG2E))
    inv = 1.0 / (total * w + total2 * w2)
    delta = (delta * w + delta2 * w2) * inv
    return w * inv, delta


def grads_kernel(meta, stats, came, p_all, dp_all, rows_qg, ks, dkv, dq_own, dq_other, dk, dv, kt, dqt):
    dk[...] = jnp.zeros((HALF, HD), F32)
    dv[...] = jnp.zeros((HALF, HD), F32)
    dqt[...] = jnp.zeros((UNITS, HD, ROWS), F32)
    for j in range(HALF // STEP):
        kt[j] = ks[j * STEP : (j + 1) * STEP, :].T

    def unit(u, carry):
        w, delta = merge(stats, came, u)

        def grad_step(i, carry):
            rows = step_rows(i)
            p = p_all[u, rows, :] * w
            ds = (p * (dp_all[u, rows, :] - delta) * SCALE).astype(BF16)
            dv[rows, :] += mm(p.astype(BF16), rows_qg[1, u])
            dk[rows, :] += mm(ds, rows_qg[0, u])
            dqt[u] += mm(kt[i], ds)
            return carry

        lax.fori_loop(0, steps_of(meta, u), grad_step, 0)
        return carry

    lax.fori_loop(0, UNITS, unit, 0)
    for i in range(OWN_BLOCKS):
        rows = slice(i * BLOCK, (i + 1) * BLOCK)
        src = block_rows(meta[i])
        dkv[rows, :HD] = dk[src, :].astype(BF16)
        dkv[rows, HD:] = dv[src, :].astype(BF16)
    for u in range(UNITS):
        dq = (dq_own, dq_other)[u // 2]
        out = dqt[u].T
        for h in range(QGROUP):
            part = (slice(u % 2 * BLOCK, (u % 2 + 1) * BLOCK), slice(h * HD, (h + 1) * HD))
            dq[part] = out[h * BLOCK : (h + 1) * BLOCK, :]


def call(kernel, ins, outs, scratch, flops, exps, args):
    space = {"s": pltpu.SMEM, "v": pltpu.VMEM}
    spec = {k: pl.BlockSpec(memory_space=m) for k, m in space.items()}
    return pl.pallas_call(
        kernel,
        out_shape=tuple(jax.ShapeDtypeStruct(shape, dtype) for _, shape, dtype in outs),
        in_specs=[spec[k] for k in ins],
        out_specs=tuple(spec[k] for k, _, _ in outs),
        scratch_shapes=[space[k](shape, dtype) for k, shape, dtype in scratch],
        compiler_params=pltpu.CompilerParams(vmem_limit_bytes=VMEM_LIMIT),
        cost_estimate=pl.CostEstimate(flops=flops, bytes_accessed=2**21, transcendentals=exps),
        name=kernel.__name__,
    )(*args)


def spread_kernel(keys, values, out, k, v, sems):
    copies = [pltpu.make_async_copy(src, dst, sems.at[i]) for i, (src, dst) in enumerate(((keys, k), (values, v)))]
    for copy in copies:
        copy.start()
    for copy in copies:
        copy.wait()
    for i in range(CHIPS):
        out[i, :, :HD] = k[...]
        out[i, :, HD:] = v[...]


def spread(keys, values):
    return pl.pallas_call(
        spread_kernel,
        out_shape=jax.ShapeDtypeStruct((CHIPS, TOK, 2 * HD), BF16),
        in_specs=[pl.BlockSpec(memory_space=pltpu.HBM)] * 2,
        out_specs=pl.BlockSpec(memory_space=pltpu.VMEM),
        scratch_shapes=[pltpu.VMEM((TOK, HD), BF16), pltpu.VMEM((TOK, HD), BF16), pltpu.SemaphoreType.DMA((2,))],
        compiler_params=pltpu.CompilerParams(vmem_limit_bytes=56 * 2**20),
        name="spread_kernel",
    )(keys, values)


def prepare(order, place, q_own, q_other, g_own, g_other):
    row = ("v", (2, UNITS, ROWS, HD), BF16)
    words = ("s", (2 * OWN_BLOCKS,), jnp.int32)
    return call(
        prep_kernel, "ssvvvv", [words, row], [words, words], 0, 0,
        (order, place, q_own, q_other, g_own, g_other),
    )


def all_grads(prepared, kv, swap):
    meta, rows_qg = prepared
    pairs = UNITS * ROWS * HALF
    table = ("v", (UNITS, HALF, ROWS), F32)
    keys = ("v", (HALF, HD), BF16)
    sums = ("v", (HALF, HD), F32)
    stats, p_all, dp_all, ks = call(
        stats_kernel, "svv", [("v", (UNITS, 8, ROWS), F32), table, table, keys], [keys],
        4 * pairs * HD, pairs, (meta, kv, rows_qg),
    )
    came = swap(stats)
    out = ("v", (TOK, QGROUP * HD), F32)
    return call(
        grads_kernel, "svvvvvv", [("v", (HALF, 2 * HD), BF16), out, out],
        [sums, sums, ("v", (HALF // STEP, HD, STEP), BF16), ("v", (UNITS, HD, ROWS), F32)],
        6 * pairs * HD, 0, (meta, stats, came, p_all, dp_all, rows_qg, ks),
    )


def shards(queries, keys, values, out_grad, block_order):
    plane = ("y", "x")

    def swap(x):
        return lax.ppermute(x, "core", [(0, 1), (1, 0)])

    q_other, g_other = swap(queries), swap(out_grad)
    kv = lax.all_to_all(spread(keys, values), plane, 0, 0, tiled=True).reshape(HALF, 2 * HD)
    place = lax.axis_index(("y", "x", "core")).astype(jnp.int32).reshape(1)
    prepared = prepare(block_order, place, queries, q_other, out_grad, g_other)
    dkv, dq_own, dq_other = all_grads(prepared, kv, swap)
    parts = lax.all_to_all(dkv.reshape(CHIPS, TOK, 2 * HD), plane, 0, 0, tiled=True)
    dq = (dq_own + swap(dq_other)).astype(BF16)
    dkv = jnp.sum(parts.astype(F32), axis=0).astype(BF16)
    mine = jnp.concatenate([dq, dkv], axis=1).reshape(8, TOK // 8, 10 * HD)
    got = lax.all_to_all(mine, "head", 0, 0, tiled=True).transpose(1, 0, 2)
    cols = [got[:, :, : 8 * HD], got[:, :, 8 * HD : 9 * HD], got[:, :, 9 * HD :]]
    return jnp.concatenate([c.reshape(TOK // 8, -1) for c in cols], axis=1)


def solution(mesh):
    split = Mesh(mesh.devices.reshape(4, 4, 2, 8), ("y", "x", "core", "head"))
    ctx = ("y", "x", "core")
    rows = P(ctx, "head")
    return jax.shard_map(
        shards,
        mesh=split,
        in_specs=(rows, rows, rows, rows, P()),
        out_specs=P(ctx + ("head",), None),
        check_vma=False,
    )
```

```python
import jax
import jax.numpy as jnp
from jax import lax
from jax.experimental import pallas as pl
from jax.experimental.pallas import tpu as pltpu
from jax.sharding import Mesh, PartitionSpec as P

HD = 128
QGROUP = 8
BLOCK = 64
TOK = 128
CHIPS = 16
HALF = CHIPS * TOK
OWN_BLOCKS = HALF // BLOCK
UNITS = 4
STEP = 1024
SEEN = OWN_BLOCKS
DIAGONAL = SEEN + UNITS
ROWS = QGROUP * BLOCK
NEG = -1e30
SCALE = HD**-0.5
LOG2E = 1.4426950408889634
BF16 = jnp.bfloat16
F32 = jnp.float32


def mm(a, b):
    return jnp.dot(a, b, preferred_element_type=F32)


def mm_t(a, b):
    return lax.dot_general(a, b, (((1,), (1,)), ((), ())), preferred_element_type=F32)


def fold(x, op):
    return op(x.reshape(x.shape[0] // 8, 8, x.shape[1]), axis=0)


def step_rows(i):
    return pl.ds(pl.multiple_of(i * STEP, STEP), STEP)


def block_rows(i):
    return pl.ds(pl.multiple_of(i * BLOCK, BLOCK), BLOCK)


def prep_kernel(order, place, q_own, q_other, g_own, g_other, meta, rows_qg, owner, upto):
    ctx = place[0]
    core = lax.rem(ctx, 2)

    def clear(p, carry):
        owner[p] = -1
        return carry

    lax.fori_loop(0, 2 * OWN_BLOCKS, clear, 0, unroll=True)
    for i in range(OWN_BLOCKS):
        owner[order[(i // 2) * 4 + core * 2 + i % 2]] = i

    def count(p, seen):
        i = owner[p]
        mine = i >= 0

        @pl.when(mine)
        def _():
            meta[i] = seen

        seen = seen + mine.astype(jnp.int32)
        upto[p] = seen
        return seen

    lax.fori_loop(0, 2 * OWN_BLOCKS, count, 0)
    for u in range(UNITS):
        block = order[(ctx + (u // 2) * (1 - 2 * core)) * 2 + u % 2]
        meta[SEEN + u] = upto[block]
        meta[DIAGONAL + u] = (owner[block] >= 0).astype(jnp.int32)
        q, g = ((q_own, g_own), (q_other, g_other))[u // 2]
        for h in range(QGROUP):
            part = (slice(u % 2 * BLOCK, (u % 2 + 1) * BLOCK), slice(h * HD, (h + 1) * HD))
            rows = slice(h * BLOCK, (h + 1) * BLOCK)
            rows_qg[0, u, rows, :] = q[part]
            rows_qg[1, u, rows, :] = g[part]


def steps_of(meta, u):
    return (meta[SEEN + u] * BLOCK + STEP - 1) // STEP


def stats_kernel(meta, kv, rows_qg, stats, p_all, dp_all, ks, vs):
    for i in range(OWN_BLOCKS):
        rows = slice(i * BLOCK, (i + 1) * BLOCK)
        dst = block_rows(meta[i])
        ks[dst, :] = kv[rows, :HD]
        vs[dst, :] = kv[rows, HD:]

    def unit(u, carry):
        steps = steps_of(meta, u)
        lane = lax.rem(lax.broadcasted_iota(jnp.int32, (1, ROWS), 1), BLOCK)
        limit = (meta[SEEN + u] - 1) * BLOCK + jnp.where(meta[DIAGONAL + u] > 0, lane, BLOCK - 1)

        def top_step(i, top):
            s = mm_t(ks[step_rows(i), :], rows_qg[0, u])
            key = lax.broadcasted_iota(jnp.int32, s.shape, 0)
            s = jnp.where(key <= limit - i * STEP, s, NEG)
            p_all[u, step_rows(i), :] = s
            return jnp.maximum(top, fold(s, jnp.max))

        top = lax.fori_loop(0, steps, top_step, jnp.full((8, ROWS), NEG, F32))
        top = jnp.max(top, axis=0, keepdims=True)

        def sum_step(i, carry):
            total, delta = carry
            rows = step_rows(i)
            dp = mm_t(vs[rows, :], rows_qg[1, u])
            p = jnp.exp2((p_all[u, rows, :] - top) * (SCALE * LOG2E))
            p_all[u, rows, :] = p
            dp_all[u, rows, :] = dp
            return (total + fold(p, jnp.sum), delta + fold(p * dp, jnp.sum))

        zero = jnp.zeros((8, ROWS), F32)
        total, delta = lax.fori_loop(0, steps, sum_step, (zero, zero))
        stats[u, 0:1, :] = top
        stats[u, 1:2, :] = jnp.sum(total, axis=0, keepdims=True)
        stats[u, 2:3, :] = jnp.sum(delta, axis=0, keepdims=True)
        stats[u, 3:8, :] = jnp.zeros((5, ROWS), F32)
        return carry

    lax.fori_loop(0, UNITS, unit, 0)


def merge(stats, came, u):
    other = lax.rem(u + 2, UNITS)
    top, total, delta = (stats[u, k : k + 1, :] for k in range(3))
    top2, total2, delta2 = (came[other, k : k + 1, :] for k in range(3))
    both = jnp.maximum(top, top2)
    w = jnp.exp2((top - both) * (SCALE * LOG2E))
    w2 = jnp.exp2((top2 - both) * (SCALE * LOG2E))
    inv = 1.0 / (total * w + total2 * w2)
    delta = (delta * w + delta2 * w2) * inv
    return w * inv, delta


def grads_kernel(meta, stats, came, p_all, dp_all, rows_qg, dkv, ds_all, dk, dv, held, sems):
    dk[...] = jnp.zeros((HALF, HD), F32)
    dv[...] = jnp.zeros((HALF, HD), F32)

    def leave(slot, u, i):
        return pltpu.make_async_copy(held.at[slot], ds_all.at[u, step_rows(i)], sems.at[slot])

    def unit(u, count):
        w, delta = merge(stats, came, u)

        def grad_step(i, count):
            slot = lax.rem(count, 2)

            @pl.when(count >= 2)
            def _():
                leave(slot, u, i).wait()

            rows = step_rows(i)
            p = p_all[u, rows, :] * w
            ds = (p * (dp_all[u, rows, :] - delta) * SCALE).astype(BF16)
            held[slot] = ds
            dv[rows, :] += mm(p.astype(BF16), rows_qg[1, u])
            dk[rows, :] += mm(ds, rows_qg[0, u])
            leave(slot, u, i).start()
            return count + 1

        return lax.fori_loop(0, steps_of(meta, u), grad_step, count)

    count = lax.fori_loop(0, UNITS, unit, 0)
    for i in range(OWN_BLOCKS):
        rows = slice(i * BLOCK, (i + 1) * BLOCK)
        src = block_rows(meta[i])
        dkv[rows, :HD] = dk[src, :].astype(BF16)
        dkv[rows, HD:] = dv[src, :].astype(BF16)
    for back in range(2):

        @pl.when(count > back)
        def _():
            leave(lax.rem(count + 1 - back, 2), 0, 0).wait()


def queries_kernel(meta, ks, ds_all, dq_own, dq_other, kt, dqt, held, sems):
    def fetch(u, i):
        rows = slice(i * STEP, (i + 1) * STEP)
        return pltpu.make_async_copy(ds_all.at[u, rows], held.at[u, rows], sems.at[u, i])

    steps = [steps_of(meta, u) for u in range(UNITS)]
    for u in range(UNITS):
        for i in range(HALF // STEP):
            pl.when(i < steps[u])(fetch(u, i).start)
    for j in range(HALF // STEP):
        kt[j] = ks[j * STEP : (j + 1) * STEP, :].T
    for u in range(UNITS):
        dqt[...] = jnp.zeros((HD, ROWS), F32)
        for i in range(HALF // STEP):

            @pl.when(i < steps[u])
            def _():
                fetch(u, i).wait()
                dqt[...] += mm(kt[i], held[u, i * STEP : (i + 1) * STEP, :])

        dq = (dq_own, dq_other)[u // 2]
        out = dqt[...].T
        for h in range(QGROUP):
            part = (slice(u % 2 * BLOCK, (u % 2 + 1) * BLOCK), slice(h * HD, (h + 1) * HD))
            dq[part] = out[h * BLOCK : (h + 1) * BLOCK, :]


def call(kernel, ins, outs, scratch, flops, exps, args, limit=10):
    space = {"s": pltpu.SMEM, "v": pltpu.VMEM, "h": pltpu.HBM}
    spec = {k: pl.BlockSpec(memory_space=m) for k, m in space.items()}
    return pl.pallas_call(
        kernel,
        out_shape=tuple(jax.ShapeDtypeStruct(shape, dtype) for _, shape, dtype in outs),
        in_specs=[spec[k] for k in ins],
        out_specs=tuple(spec[k] for k, _, _ in outs),
        scratch_shapes=[
            pltpu.SemaphoreType.DMA(shape) if k == "d" else space[k](shape, dtype) for k, shape, dtype in scratch
        ],
        compiler_params=pltpu.CompilerParams(vmem_limit_bytes=limit * 2**20),
        cost_estimate=pl.CostEstimate(flops=flops, bytes_accessed=2**21, transcendentals=exps),
        name=kernel.__name__,
    )(*args)


def spread_kernel(keys, values, out, k, v, sems):
    copies = [pltpu.make_async_copy(src, dst, sems.at[i]) for i, (src, dst) in enumerate(((keys, k), (values, v)))]
    for copy in copies:
        copy.start()
    for copy in copies:
        copy.wait()
    for i in range(CHIPS):
        out[i, :, :HD] = k[...]
        out[i, :, HD:] = v[...]


def spread(keys, values):
    return pl.pallas_call(
        spread_kernel,
        out_shape=jax.ShapeDtypeStruct((CHIPS, TOK, 2 * HD), BF16),
        in_specs=[pl.BlockSpec(memory_space=pltpu.HBM)] * 2,
        out_specs=pl.BlockSpec(memory_space=pltpu.VMEM),
        scratch_shapes=[pltpu.VMEM((TOK, HD), BF16), pltpu.VMEM((TOK, HD), BF16), pltpu.SemaphoreType.DMA((2,))],
        compiler_params=pltpu.CompilerParams(vmem_limit_bytes=56 * 2**20),
        name="spread_kernel",
    )(keys, values)


def prepare(order, place, q_own, q_other, g_own, g_other):
    row = ("v", (2, UNITS, ROWS, HD), BF16)
    words = ("s", (2 * OWN_BLOCKS,), jnp.int32)
    return call(
        prep_kernel, "ssvvvv", [words, row], [words, words], 0, 0,
        (order, place, q_own, q_other, g_own, g_other),
    )


def key_grads(prepared, kv, swap):
    meta, rows_qg = prepared
    pairs = UNITS * ROWS * HALF
    table = ("v", (UNITS, HALF, ROWS), F32)
    keys = ("v", (HALF, HD), BF16)
    sums = ("v", (HALF, HD), F32)
    stats, p_all, dp_all, ks = call(
        stats_kernel, "svv", [("v", (UNITS, 8, ROWS), F32), table, table, keys], [keys],
        4 * pairs * HD, pairs, (meta, kv, rows_qg),
    )
    came = swap(stats)
    dkv, ds_all = call(
        grads_kernel, "svvvvv", [("v", (HALF, 2 * HD), BF16), ("h", (4 * UNITS, HALF, ROWS), BF16)],
        [sums, sums, ("v", (2, STEP, ROWS), BF16), ("d", (2,), None)],
        4 * pairs * HD, 0, (meta, stats, came, p_all, dp_all, rows_qg),
    )
    return dkv, ks, ds_all


def query_grads(meta, ks, ds_all):
    out = ("v", (TOK, QGROUP * HD), F32)
    scratch = [
        ("v", (HALF // STEP, HD, STEP), BF16),
        ("v", (HD, ROWS), F32),
        ("v", (UNITS, HALF, ROWS), BF16),
        ("d", (UNITS, HALF // STEP), None),
    ]
    return call(
        queries_kernel, "svh", [out, out], scratch, 2 * UNITS * ROWS * HALF * HD, 0, (meta, ks, ds_all), 40
    )


def shards(queries, keys, values, out_grad, block_order):
    plane = ("y", "x")

    def swap(x):
        return lax.ppermute(x, "core", [(0, 1), (1, 0)])

    q_other, g_other = swap(queries), swap(out_grad)
    kv = lax.all_to_all(spread(keys, values), plane, 0, 0, tiled=True).reshape(HALF, 2 * HD)
    place = lax.axis_index(("y", "x", "core")).astype(jnp.int32).reshape(1)
    prepared = prepare(block_order, place, queries, q_other, out_grad, g_other)
    dkv, ks, ds_all = key_grads(prepared, kv, swap)
    parts = lax.all_to_all(dkv.reshape(CHIPS, TOK, 2 * HD), plane, 0, 0, tiled=True)
    dq_own, dq_other = query_grads(prepared[0], ks, ds_all)
    dq = (dq_own + swap(dq_other)).astype(BF16)
    dkv = jnp.sum(parts.astype(F32), axis=0).astype(BF16)
    mine = jnp.concatenate([dq, dkv], axis=1).reshape(8, TOK // 8, 10 * HD)
    got = lax.all_to_all(mine, "head", 0, 0, tiled=True).transpose(1, 0, 2)
    cols = [got[:, :, : 8 * HD], got[:, :, 8 * HD : 9 * HD], got[:, :, 9 * HD :]]
    return jnp.concatenate([c.reshape(TOK // 8, -1) for c in cols], axis=1)


def solution(mesh):
    split = Mesh(mesh.devices.reshape(4, 4, 2, 8), ("y", "x", "core", "head"))
    ctx = ("y", "x", "core")
    rows = P(ctx, "head")
    return jax.shard_map(
        shards,
        mesh=split,
        in_specs=(rows, rows, rows, rows, P()),
        out_specs=P(ctx + ("head",), None),
        check_vma=False,
    )
```

```python
import jax
import jax.numpy as jnp
from jax import lax
from jax.experimental import pallas as pl
from jax.experimental.pallas import tpu as pltpu
from jax.sharding import Mesh, PartitionSpec as P

HD = 128
QGROUP = 8
BLOCK = 64
TOK = 128
CHIPS = 16
HALF = CHIPS * TOK
OWN_BLOCKS = HALF // BLOCK
UNITS = 4
STEP = 1024
SEEN = OWN_BLOCKS
DIAGONAL = SEEN + UNITS
PLACE = DIAGONAL + UNITS
ROWS = QGROUP * BLOCK
NEG = -1e30
SCALE = HD**-0.5
LOG2E = 1.4426950408889634
BF16 = jnp.bfloat16
F32 = jnp.float32


def mm(a, b):
    return jnp.dot(a, b, preferred_element_type=F32)


def mm_t(a, b):
    return lax.dot_general(a, b, (((1,), (1,)), ((), ())), preferred_element_type=F32)


def fold(x, op):
    return op(x.reshape(x.shape[0] // 8, 8, x.shape[1]), axis=0)


def step_rows(i):
    return pl.ds(pl.multiple_of(i * STEP, STEP), STEP)


def block_rows(i):
    return pl.ds(pl.multiple_of(i * BLOCK, BLOCK), BLOCK)


def prep_kernel(order, place, q_own, q_other, g_own, g_other, meta, rows_qg, owner, upto):
    ctx = place[0]
    core = lax.rem(ctx, 2)
    meta[PLACE] = ctx

    def clear(p, carry):
        owner[p] = -1
        return carry

    lax.fori_loop(0, 2 * OWN_BLOCKS, clear, 0, unroll=True)
    for i in range(OWN_BLOCKS):
        owner[order[(i // 2) * 4 + core * 2 + i % 2]] = i

    def count(p, seen):
        i = owner[p]
        mine = i >= 0

        @pl.when(mine)
        def _():
            meta[i] = seen

        seen = seen + mine.astype(jnp.int32)
        upto[p] = seen
        return seen

    lax.fori_loop(0, 2 * OWN_BLOCKS, count, 0)
    for u in range(UNITS):
        block = order[(ctx + (u // 2) * (1 - 2 * core)) * 2 + u % 2]
        meta[SEEN + u] = upto[block]
        meta[DIAGONAL + u] = (owner[block] >= 0).astype(jnp.int32)
        q, g = ((q_own, g_own), (q_other, g_other))[u // 2]
        for h in range(QGROUP):
            part = (slice(u % 2 * BLOCK, (u % 2 + 1) * BLOCK), slice(h * HD, (h + 1) * HD))
            rows = slice(h * BLOCK, (h + 1) * BLOCK)
            rows_qg[0, u, rows, :] = q[part]
            rows_qg[1, u, rows, :] = g[part]


def steps_of(meta, u):
    return (meta[SEEN + u] * BLOCK + STEP - 1) // STEP


def stats_kernel(meta, k0, k1, k2, k3, v0, v1, v2, v3, rows_qg, stats, p_all, dp_all, ks, vs):
    y, x = meta[PLACE] // 8, lax.rem(meta[PLACE] // 2, 4)
    for dy in range(4):
        for dx in range(4):
            chip = lax.rem(y + 4 - dy, 4) * 4 + lax.rem(x + 4 - dx, 4)
            for h in range(2):
                dst = block_rows(meta[chip * 2 + h])
                ks[dst, :] = (k0, k1, k2, k3)[dy][dx * TOK + h * BLOCK : dx * TOK + (h + 1) * BLOCK, :]
                vs[dst, :] = (v0, v1, v2, v3)[dx][dy * TOK + h * BLOCK : dy * TOK + (h + 1) * BLOCK, :]

    def unit(u, carry):
        steps = steps_of(meta, u)
        lane = lax.rem(lax.broadcasted_iota(jnp.int32, (1, ROWS), 1), BLOCK)
        limit = (meta[SEEN + u] - 1) * BLOCK + jnp.where(meta[DIAGONAL + u] > 0, lane, BLOCK - 1)

        def top_step(i, top):
            s = mm_t(ks[step_rows(i), :], rows_qg[0, u])
            key = lax.broadcasted_iota(jnp.int32, s.shape, 0)
            s = jnp.where(key <= limit - i * STEP, s, NEG)
            p_all[u, step_rows(i), :] = s
            return jnp.maximum(top, fold(s, jnp.max))

        top = lax.fori_loop(0, steps, top_step, jnp.full((8, ROWS), NEG, F32))
        top = jnp.max(top, axis=0, keepdims=True)

        def sum_step(i, carry):
            total, delta = carry
            rows = step_rows(i)
            dp = mm_t(vs[rows, :], rows_qg[1, u])
            p = jnp.exp2((p_all[u, rows, :] - top) * (SCALE * LOG2E))
            p_all[u, rows, :] = p
            dp_all[u, rows, :] = dp
            return (total + fold(p, jnp.sum), delta + fold(p * dp, jnp.sum))

        zero = jnp.zeros((8, ROWS), F32)
        total, delta = lax.fori_loop(0, steps, sum_step, (zero, zero))
        stats[u, 0:1, :] = top
        stats[u, 1:2, :] = jnp.sum(total, axis=0, keepdims=True)
        stats[u, 2:3, :] = jnp.sum(delta, axis=0, keepdims=True)
        stats[u, 3:8, :] = jnp.zeros((5, ROWS), F32)
        return carry

    lax.fori_loop(0, UNITS, unit, 0)


def merge(stats, came, u):
    other = lax.rem(u + 2, UNITS)
    top, total, delta = (stats[u, k : k + 1, :] for k in range(3))
    top2, total2, delta2 = (came[other, k : k + 1, :] for k in range(3))
    both = jnp.maximum(top, top2)
    w = jnp.exp2((top - both) * (SCALE * LOG2E))
    w2 = jnp.exp2((top2 - both) * (SCALE * LOG2E))
    inv = 1.0 / (total * w + total2 * w2)
    delta = (delta * w + delta2 * w2) * inv
    return w * inv, delta


def grads_kernel(meta, stats, came, p_all, dp_all, rows_qg, dkv, ds_all, dk, dv, held, sems):
    dk[...] = jnp.zeros((HALF, HD), F32)
    dv[...] = jnp.zeros((HALF, HD), F32)

    def leave(slot, u, i):
        return pltpu.make_async_copy(held.at[slot], ds_all.at[u, step_rows(i)], sems.at[slot])

    def unit(u, count):
        w, delta = merge(stats, came, u)

        def grad_step(i, count):
            slot = lax.rem(count, 2)

            @pl.when(count >= 2)
            def _():
                leave(slot, u, i).wait()

            rows = step_rows(i)
            p = p_all[u, rows, :] * w
            ds = (p * (dp_all[u, rows, :] - delta)).astype(BF16)
            held[slot] = ds
            dv[rows, :] += mm(p.astype(BF16), rows_qg[1, u])
            dk[rows, :] += mm(ds, rows_qg[0, u])
            leave(slot, u, i).start()
            return count + 1

        return lax.fori_loop(0, steps_of(meta, u), grad_step, count)

    count = lax.fori_loop(0, UNITS, unit, 0)
    for i in range(OWN_BLOCKS):
        rows = slice(i * BLOCK, (i + 1) * BLOCK)
        src = block_rows(meta[i])
        dkv[rows, :HD] = (dk[src, :] * SCALE).astype(BF16)
        dkv[rows, HD:] = dv[src, :].astype(BF16)
    for back in range(2):

        @pl.when(count > back)
        def _():
            leave(lax.rem(count + 1 - back, 2), 0, 0).wait()


def queries_kernel(meta, ks, ds_all, dq_own, dq_other, kt, dqt, held, sems):
    def fetch(u, i):
        rows = slice(i * STEP, (i + 1) * STEP)
        return pltpu.make_async_copy(ds_all.at[u, rows], held.at[u, rows], sems.at[u, i])

    steps = [steps_of(meta, u) for u in range(UNITS)]
    for u in range(UNITS):
        for i in range(HALF // STEP):
            pl.when(i < steps[u])(fetch(u, i).start)
    for j in range(HALF // STEP):
        kt[j] = ks[j * STEP : (j + 1) * STEP, :].T
    for u in range(UNITS):
        dqt[...] = jnp.zeros((HD, ROWS), F32)
        for i in range(HALF // STEP):

            @pl.when(i < steps[u])
            def _():
                fetch(u, i).wait()
                dqt[...] += mm(kt[i], held[u, i * STEP : (i + 1) * STEP, :])

        dq = (dq_own, dq_other)[u // 2]
        out = dqt[...].T * SCALE
        for h in range(QGROUP):
            part = (slice(u % 2 * BLOCK, (u % 2 + 1) * BLOCK), slice(h * HD, (h + 1) * HD))
            dq[part] = out[h * BLOCK : (h + 1) * BLOCK, :]


def call(kernel, ins, outs, scratch, flops, exps, args, limit=10):
    space = {"s": pltpu.SMEM, "v": pltpu.VMEM, "h": pltpu.HBM}
    spec = {k: pl.BlockSpec(memory_space=m) for k, m in space.items()}
    return pl.pallas_call(
        kernel,
        out_shape=tuple(jax.ShapeDtypeStruct(shape, dtype) for _, shape, dtype in outs),
        in_specs=[spec[k] for k in ins],
        out_specs=tuple(spec[k] for k, _, _ in outs),
        scratch_shapes=[
            pltpu.SemaphoreType.DMA(shape) if k == "d" else space[k](shape, dtype) for k, shape, dtype in scratch
        ],
        compiler_params=pltpu.CompilerParams(vmem_limit_bytes=limit * 2**20),
        cost_estimate=pl.CostEstimate(flops=flops, bytes_accessed=2**21, transcendentals=exps),
        name=kernel.__name__,
    )(*args)


def join_kernel(k0, k1, k2, k3, v0, v1, v2, v3, k, v):
    for out, parts in ((k, (k0, k1, k2, k3)), (v, (v0, v1, v2, v3))):
        for i, part in enumerate(parts):
            out[i * TOK : (i + 1) * TOK, :] = part[...]


def gather(keys, values):
    def shifts(v, axis):
        moved = {s: lax.ppermute(v, axis, [(i, (i + s) % 4) for i in range(4)]) for s in (2, 1, 3)}
        return (v, moved[1], moved[2], moved[3])

    line = ("v", (4 * TOK, HD), BF16)
    k, v = call(join_kernel, "v" * 8, [line, line], [], 0, 0, shifts(keys, "x") + shifts(values, "y"))
    return shifts(k, "y") + shifts(v, "x")


def prepare(order, place, q_own, q_other, g_own, g_other):
    row = ("v", (2, UNITS, ROWS, HD), BF16)
    words = ("s", (2 * OWN_BLOCKS,), jnp.int32)
    return call(
        prep_kernel, "ssvvvv", [words, row], [words, words], 0, 0,
        (order, place, q_own, q_other, g_own, g_other),
    )


def key_grads(prepared, kv, swap):
    meta, rows_qg = prepared
    pairs = UNITS * ROWS * HALF
    table = ("v", (UNITS, HALF, ROWS), F32)
    keys = ("v", (HALF, HD), BF16)
    sums = ("v", (HALF, HD), F32)
    stats, p_all, dp_all, ks = call(
        stats_kernel, "s" + 9 * "v", [("v", (UNITS, 8, ROWS), F32), table, table, keys], [keys],
        4 * pairs * HD, pairs, (meta, *kv, rows_qg),
    )
    came = swap(stats)
    dkv, ds_all = call(
        grads_kernel, "svvvvv", [("v", (HALF, 2 * HD), BF16), ("h", (4 * UNITS, HALF, ROWS), BF16)],
        [sums, sums, ("v", (2, STEP, ROWS), BF16), ("d", (2,), None)],
        4 * pairs * HD, 0, (meta, stats, came, p_all, dp_all, rows_qg),
    )
    return dkv, ks, ds_all


def query_grads(meta, ks, ds_all):
    out = ("v", (TOK, QGROUP * HD), F32)
    scratch = [
        ("v", (HALF // STEP, HD, STEP), BF16),
        ("v", (HD, ROWS), F32),
        ("v", (UNITS, HALF, ROWS), BF16),
        ("d", (UNITS, HALF // STEP), None),
    ]
    return call(
        queries_kernel, "svh", [out, out], scratch, 2 * UNITS * ROWS * HALF * HD, 0, (meta, ks, ds_all), 40
    )


def shards(queries, keys, values, out_grad, block_order):
    plane = ("y", "x")

    def swap(x):
        return lax.ppermute(x, "core", [(0, 1), (1, 0)])

    q_other, g_other = swap(queries), swap(out_grad)
    kv = gather(keys, values)
    place = lax.axis_index(("y", "x", "core")).astype(jnp.int32).reshape(1)
    prepared = prepare(block_order, place, queries, q_other, out_grad, g_other)
    dkv, ks, ds_all = key_grads(prepared, kv, swap)
    parts = lax.all_to_all(dkv.reshape(CHIPS, TOK, 2 * HD), plane, 0, 0, tiled=True)
    dq_own, dq_other = query_grads(prepared[0], ks, ds_all)
    dq = (dq_own + swap(dq_other)).astype(BF16)
    dkv = jnp.sum(parts.astype(F32), axis=0).astype(BF16)
    mine = jnp.concatenate([dq, dkv], axis=1).reshape(8, TOK // 8, 10 * HD)
    got = lax.all_to_all(mine, "head", 0, 0, tiled=True).transpose(1, 0, 2)
    cols = [got[:, :, : 8 * HD], got[:, :, 8 * HD : 9 * HD], got[:, :, 9 * HD :]]
    return jnp.concatenate([c.reshape(TOK // 8, -1) for c in cols], axis=1)


def solution(mesh):
    split = Mesh(mesh.devices.reshape(4, 4, 2, 8), ("y", "x", "core", "head"))
    ctx = ("y", "x", "core")
    rows = P(ctx, "head")
    return jax.shard_map(
        shards,
        mesh=split,
        in_specs=(rows, rows, rows, rows, P()),
        out_specs=P(ctx + ("head",), None),
        check_vma=False,
    )
```

```python
import jax
import jax.numpy as jnp
from jax import lax
from jax.experimental import pallas as pl
from jax.experimental.pallas import tpu as pltpu
from jax.sharding import Mesh, PartitionSpec as P

HD = 128
QGROUP = 8
BLOCK = 64
TOK = 128
UNITS = 4
ROWS = QGROUP * BLOCK
ALL_ROWS = UNITS * ROWS
LINE = 4 * TOK
LANES = 1024
NEG = -1e30
SCALE = HD**-0.5
LOG2E = 1.4426950408889634
QUERY = 32
BF16 = jnp.bfloat16
F32 = jnp.float32


def mm(a, b):
    return jnp.dot(a, b, preferred_element_type=F32)


def mm_t(a, b):
    return lax.dot_general(a, b, (((1,), (1,)), ((), ())), preferred_element_type=F32)


def fold(x, op):
    return op(op(x.reshape(x.shape[0] // 8, 8, x.shape[1]), axis=0), axis=0, keepdims=True)


def call(kernel, name, ins, outs, scratch, flops, exps, args, limit=10):
    space = {"s": pltpu.SMEM, "v": pltpu.VMEM}
    spec = {k: pl.BlockSpec(memory_space=m) for k, m in space.items()}
    return pl.pallas_call(
        kernel,
        out_shape=tuple(jax.ShapeDtypeStruct(shape, dtype) for _, shape, dtype in outs),
        in_specs=[spec[k] for k in ins],
        out_specs=tuple(spec[k] for k, _, _ in outs),
        scratch_shapes=[space[k](shape, dtype) for k, shape, dtype in scratch],
        compiler_params=pltpu.CompilerParams(vmem_limit_bytes=limit * 2**20),
        cost_estimate=pl.CostEstimate(flops=flops, bytes_accessed=2**20, transcendentals=exps),
        name=name,
    )(*args)


def join(parts):
    def kernel(*refs):
        for i, part in enumerate(refs[:-1]):
            refs[-1][i * TOK : (i + 1) * TOK, :] = part[...]

    return call(kernel, "join", "v" * 4, [("v", (LINE, 2 * HD), BF16)], [], 0, 0, parts)[0]


def prep_kernel(order, place, q_own, q_other, g_own, g_other, meta, rows_qg):
    ctx = place[0]
    core, x, y = lax.rem(ctx, 2), lax.rem(ctx // 2, 4), ctx // 8
    for dy in range(4):
        for dx in range(4):
            chip = lax.rem(y + 4 - dy, 4) * 4 + lax.rem(x + 4 - dx, 4)
            for h in range(2):
                meta[dy * 8 + dx * 2 + h] = order[(chip * 2 + core) * 2 + h]
    for u in range(UNITS):
        meta[QUERY + u] = order[(ctx + (u // 2) * (1 - 2 * core)) * 2 + u % 2]
        q, g = ((q_own, g_own), (q_other, g_other))[u // 2]
        for h in range(QGROUP):
            part = (slice(u % 2 * BLOCK, (u % 2 + 1) * BLOCK), slice(h * HD, (h + 1) * HD))
            rows = slice(u * ROWS + h * BLOCK, u * ROWS + (h + 1) * BLOCK)
            rows_qg[0, rows, :] = q[part]
            rows_qg[1, rows, :] = g[part]


def prepare(order, place, q_own, q_other, g_own, g_other):
    outs = [("s", (QUERY + UNITS,), jnp.int32), ("v", (2, ALL_ROWS, HD), BF16)]
    return call(
        prep_kernel, "prep", "ssvvvv", outs, [], 0, 0, (order, place, q_own, q_other, g_own, g_other)
    )


def merge(a, b):
    top = jnp.maximum(a[0], b[0])
    wa, wb = jnp.exp2(a[0] - top), jnp.exp2(b[0] - top)
    return top, a[1] * wa + b[1] * wb, a[2] * wa + b[2] * wb


def stats_of(ref, lanes=slice(None)):
    return tuple(ref[k : k + 1, lanes] for k in range(3))


def stats_piece(dy, meta, rows_qg, lines, before):
    chunks = len(lines)

    def kernel(meta, rows_qg, *refs):
        lines = refs[:chunks]
        before = refs[chunks] if len(refs) > chunks + 3 else None
        stats, p_all, dp_all = refs[-3:]
        stats[...] = jnp.zeros((8, ALL_ROWS), F32)
        size = LINE // chunks
        for half in range(ALL_ROWS // LANES):
            lanes = slice(half * LANES, (half + 1) * LANES)
            lane = lax.broadcasted_iota(jnp.int32, (1, LANES), 1)
            first, second = meta[QUERY + half * 2], meta[QUERY + half * 2 + 1]
            row_pos = jnp.where(lane < ROWS, first, second) * BLOCK + lax.rem(lane, BLOCK)
            key = lax.broadcasted_iota(jnp.int32, (BLOCK, LANES), 0)
            tops = []
            for c, line in enumerate(lines):
                s = mm_t(line[:, :HD], rows_qg[0, lanes, :]) * (SCALE * LOG2E)
                for b in range(size // BLOCK):
                    base = meta[dy * 8 + c * (size // BLOCK) + b] * BLOCK
                    part = jnp.where(key <= row_pos - base, s[b * BLOCK : (b + 1) * BLOCK], NEG)
                    p_all[c * size + b * BLOCK : c * size + (b + 1) * BLOCK, lanes] = part
                    tops.append(jnp.max(part.reshape(8, 8, LANES), axis=0))
            while len(tops) > 1:
                tops = [jnp.maximum(tops[i], tops[i + 1]) for i in range(0, len(tops), 2)]
            top = jnp.max(tops[0], axis=0, keepdims=True)
            total, delta = jnp.zeros((1, LANES), F32), jnp.zeros((1, LANES), F32)
            for c, line in enumerate(lines):
                rows = slice(c * size, (c + 1) * size)
                dp = mm_t(line[:, HD:], rows_qg[1, lanes, :])
                p = jnp.exp2(p_all[rows, lanes] - top)
                p_all[rows, lanes] = p
                dp_all[rows, lanes] = dp
                total += fold(p, jnp.sum)
                delta += fold(p * dp, jnp.sum)
            stats[3:4, lanes] = top
            now = (top, total, delta)
            if before is not None:
                now = merge(stats_of(before, lanes), now)
            for k in range(3):
                stats[k : k + 1, lanes] = now[k]

    table = ("v", (LINE, ALL_ROWS), F32)
    args = (meta, rows_qg, *lines) + (() if before is None else (before,))
    pairs = LINE * ALL_ROWS
    return call(
        kernel, "stats", "s" + "v" * (len(args) - 1), [("v", (8, ALL_ROWS), F32), table, table], [],
        4 * pairs * HD, pairs, args,
    )


def swapped(came):
    halves = [stats_of(came, slice(h * LANES, (h + 1) * LANES)) for h in (1, 0)]
    return tuple(jnp.concatenate(pair, axis=1) for pair in zip(*halves))


def weights(own, final, came):
    top, total, delta = merge(stats_of(final), swapped(came))
    inv = 1.0 / total
    return jnp.exp2(own[3:4, :] - top) * inv, delta * inv


def grads_piece(rows_qg, piece, final, came, pieces, dtype):
    size = LINE // pieces

    def kernel(rows_qg, own, p_all, dp_all, final, came, *outs):
        w, delta = weights(own, final, came)
        step = 256
        for i in range(LINE // step):
            rows = slice(i * step, (i + 1) * step)
            p = p_all[rows, :] * w
            ds = (p * (dp_all[rows, :] - delta) * SCALE).astype(BF16)
            at = i * step // size
            dst = slice(i * step - at * size, (i + 1) * step - at * size)
            outs[at][dst, HD:] = mm(p.astype(BF16), rows_qg[1]).astype(dtype)
            outs[at][dst, :HD] = mm(ds, rows_qg[0]).astype(dtype)

    outs = [("v", (size, 2 * HD), dtype)] * pieces
    return call(
        kernel, "grads", "v" * 6, outs, [], 4 * LINE * ALL_ROWS * HD, 0, (rows_qg, *piece, final, came)
    )


def add_far(a, b, to_a, to_b):
    half = LINE // 2

    def kernel(a, b, to_a, to_b, out_a, out_b):
        out_a[:half] = a[:half].astype(BF16)
        out_a[half:] = (a[half:] + to_a[...].astype(F32)).astype(BF16)
        out_b[:half] = (b[:half] + to_b[...].astype(F32)).astype(BF16)
        out_b[half:] = b[half:].astype(BF16)

    line = ("v", (LINE, 2 * HD), BF16)
    return call(kernel, "add_far", "v" * 4, [line, line], [], 0, 0, (a, b, to_a, to_b))


def add_near(own, a, b):
    def kernel(own, a, b, *outs):
        for i, out in enumerate(outs):
            rows = slice(i * TOK, (i + 1) * TOK)
            out[...] = (own[rows, :] + a[rows, :].astype(F32) + b[rows, :].astype(F32)).astype(BF16)

    return call(kernel, "add_near", "v" * 3, [("v", (TOK, 2 * HD), BF16)] * 4, [], 0, 0, (own, a, b))


def query_grads(lines, pieces, final, came):
    counts = [len(group) for group in lines]

    def kernel(final, came, *refs):
        dq_own, dq_other, kt, dqt = refs[-4:]
        refs = list(refs[:-4])
        groups = [[refs.pop(0) for _ in range(n)] for n in counts]
        tables = [[refs.pop(0) for _ in range(3)] for _ in counts]
        for j, group in enumerate(groups):
            size = LINE // len(group)
            for c, line in enumerate(group):
                kt[j, :, c * size : (c + 1) * size] = line[:, :HD].T
        for half in range(ALL_ROWS // LANES):
            lanes = slice(half * LANES, (half + 1) * LANES)
            theirs = slice((1 - half) * LANES, (2 - half) * LANES)
            top, total, delta = merge(stats_of(final, lanes), stats_of(came, theirs))
            inv = 1.0 / total
            delta = delta * inv
            for j, (own, p_all, dp_all) in enumerate(tables):
                w = jnp.exp2(own[3:4, lanes] - top) * inv
                ds = (p_all[:, lanes] * w * (dp_all[:, lanes] - delta) * SCALE).astype(BF16)
                part = mm(kt[j], ds)
                dqt[...] = part if j == 0 else dqt[...] + part
            out = dqt[...].T
            for u in range(2):
                for h in range(QGROUP):
                    part = (slice(u * BLOCK, (u + 1) * BLOCK), slice(h * HD, (h + 1) * HD))
                    rows = slice(u * ROWS + h * BLOCK, u * ROWS + (h + 1) * BLOCK)
                    (dq_own, dq_other)[half][part] = out[rows, :]

    args = (final, came) + tuple(x for group in lines for x in group) + tuple(x for piece in pieces for x in piece)
    out = ("v", (TOK, QGROUP * HD), F32)
    scratch = [("v", (4, HD, LINE), BF16), ("v", (HD, LANES), F32)]
    return call(
        kernel, "queries", "v" * len(args), [out, out], scratch, 8 * LINE * ALL_ROWS * HD, 0, args
    )


def shards(queries, keys, values, out_grad, block_order):
    def swap(x):
        return lax.ppermute(x, "core", [(0, 1), (1, 0)])

    def shift(x, axis, s):
        return lax.ppermute(x, axis, [(i, (i + s) % 4) for i in range(4)])

    kv = jnp.concatenate([keys, values], axis=1)
    line = join((kv, shift(kv, "x", 1), shift(kv, "x", 2), shift(kv, "x", 3)))
    up, down = shift(line, "y", 1), shift(line, "y", 3)
    far = (shift(down[: LINE // 2], "y", 3), shift(up[LINE // 2 :], "y", 1))
    place = lax.axis_index(("y", "x", "core")).astype(jnp.int32).reshape(1)
    meta, rows_qg = prepare(block_order, place, queries, swap(queries), out_grad, swap(out_grad))
    lines = ((line,), (up,), (down,), far)
    pieces, before = [], None
    for dy, group in zip((0, 1, 3, 2), lines):
        pieces.append(stats_piece(dy, meta, rows_qg, group, before))
        before = pieces[-1][0]
    came = swap(before)
    far1, far2 = grads_piece(rows_qg, pieces[3], before, came, 2, BF16)
    (up_part,) = grads_piece(rows_qg, pieces[1], before, came, 1, F32)
    (down_part,) = grads_piece(rows_qg, pieces[2], before, came, 1, F32)
    up_sum, down_sum = add_far(up_part, down_part, shift(far2, "y", 3), shift(far1, "y", 1))
    (own_part,) = grads_piece(rows_qg, pieces[0], before, came, 1, F32)
    parts = add_near(own_part, shift(up_sum, "y", 3), shift(down_sum, "y", 1))
    dq_own, dq_other = query_grads(lines, pieces, before, came)
    dq = (dq_own + swap(dq_other)).astype(BF16)
    dkv = parts[0].astype(F32)
    for s in (1, 2, 3):
        dkv = dkv + shift(parts[s], "x", 4 - s).astype(F32)
    mine = jnp.concatenate([dq, dkv.astype(BF16)], axis=1).reshape(8, TOK // 8, 10 * HD)
    got = lax.all_to_all(mine, "head", 0, 0, tiled=True).transpose(1, 0, 2)
    cols = [got[:, :, : 8 * HD], got[:, :, 8 * HD : 9 * HD], got[:, :, 9 * HD :]]
    return jnp.concatenate([c.reshape(TOK // 8, -1) for c in cols], axis=1)


def solution(mesh):
    split = Mesh(mesh.devices.reshape(4, 4, 2, 8), ("y", "x", "core", "head"))
    ctx = ("y", "x", "core")
    rows = P(ctx, "head")
    return jax.shard_map(
        shards,
        mesh=split,
        in_specs=(rows, rows, rows, rows, P()),
        out_specs=P(ctx + ("head",), None),
        check_vma=False,
    )
```

```python
import jax
import jax.numpy as jnp
from jax import lax
from jax.experimental import pallas as pl
from jax.experimental.pallas import tpu as pltpu
from jax.sharding import Mesh, PartitionSpec as P

HD = 128
QGROUP = 8
BLOCK = 64
TOK = 128
UNITS = 4
ROWS = QGROUP * BLOCK
ALL_ROWS = UNITS * ROWS
LINE = 4 * TOK
LANES = 1024
NEG = -1e30
SCALE = HD**-0.5
LOG2E = 1.4426950408889634
QUERY = 32
BF16 = jnp.bfloat16
F32 = jnp.float32


def mm(a, b):
    return jnp.dot(a, b, preferred_element_type=F32)


def mm_t(a, b):
    return lax.dot_general(a, b, (((1,), (1,)), ((), ())), preferred_element_type=F32)


def fold(x, op):
    return op(op(x.reshape(x.shape[0] // 8, 8, x.shape[1]), axis=0), axis=0, keepdims=True)


def call(kernel, name, ins, outs, scratch, flops, exps, args, limit=10):
    space = {"s": pltpu.SMEM, "v": pltpu.VMEM}
    spec = {k: pl.BlockSpec(memory_space=m) for k, m in space.items()}
    return pl.pallas_call(
        kernel,
        out_shape=tuple(jax.ShapeDtypeStruct(shape, dtype) for _, shape, dtype in outs),
        in_specs=[spec[k] for k in ins],
        out_specs=tuple(spec[k] for k, _, _ in outs),
        scratch_shapes=[space[k](shape, dtype) for k, shape, dtype in scratch],
        compiler_params=pltpu.CompilerParams(vmem_limit_bytes=limit * 2**20),
        cost_estimate=pl.CostEstimate(flops=flops, bytes_accessed=2**20, transcendentals=exps),
        name=name,
    )(*args)


def join(parts):
    def kernel(*refs):
        for i, part in enumerate(refs[:-1]):
            refs[-1][i * TOK : (i + 1) * TOK, :] = part[...]

    return call(kernel, "join", "v" * 4, [("v", (LINE, 2 * HD), BF16)], [], 0, 0, parts)[0]


def prep_kernel(order, place, q_own, q_other, g_own, g_other, meta, rows_qg):
    ctx = place[0]
    core, x, y = lax.rem(ctx, 2), lax.rem(ctx // 2, 4), ctx // 8
    for dy in range(4):
        for dx in range(4):
            chip = lax.rem(y + 4 - dy, 4) * 4 + lax.rem(x + 4 - dx, 4)
            for h in range(2):
                meta[dy * 8 + dx * 2 + h] = order[(chip * 2 + core) * 2 + h]
    for u in range(UNITS):
        meta[QUERY + u] = order[(ctx + (u // 2) * (1 - 2 * core)) * 2 + u % 2]
        q, g = ((q_own, g_own), (q_other, g_other))[u // 2]
        for h in range(QGROUP):
            part = (slice(u % 2 * BLOCK, (u % 2 + 1) * BLOCK), slice(h * HD, (h + 1) * HD))
            rows = slice(u * ROWS + h * BLOCK, u * ROWS + (h + 1) * BLOCK)
            rows_qg[0, rows, :] = q[part]
            rows_qg[1, rows, :] = g[part]


def prepare(order, place, q_own, q_other, g_own, g_other):
    outs = [("s", (QUERY + UNITS,), jnp.int32), ("v", (2, ALL_ROWS, HD), BF16)]
    return call(
        prep_kernel, "prep", "ssvvvv", outs, [], 0, 0, (order, place, q_own, q_other, g_own, g_other)
    )


def merge(a, b):
    top = jnp.maximum(a[0], b[0])
    wa, wb = jnp.exp2(a[0] - top), jnp.exp2(b[0] - top)
    return top, a[1] * wa + b[1] * wb, a[2] * wa + b[2] * wb


def stats_of(ref, lanes=slice(None)):
    return tuple(ref[k : k + 1, lanes] for k in range(3))


def stats_piece(dy, meta, rows_qg, lines, before):
    chunks = len(lines)

    def kernel(meta, rows_qg, *refs):
        lines = refs[:chunks]
        before = refs[chunks] if len(refs) > chunks + 3 else None
        stats, p_all, dp_all = refs[-3:]
        stats[...] = jnp.zeros((8, ALL_ROWS), F32)
        size = LINE // chunks
        def bias(half, kb):
            base = meta[dy * 8 + kb]
            cost = [jnp.where(base <= meta[QUERY + half * 2 + u], 0.0, -NEG).astype(F32) for u in range(2)]
            lane = lax.broadcasted_iota(jnp.int32, (1, LANES), 1)
            return jnp.where(lane < ROWS, cost[0], cost[1])

        for half in range(ALL_ROWS // LANES):
            lanes = slice(half * LANES, (half + 1) * LANES)
            biases = [bias(half, kb) for kb in range(LINE // BLOCK)]
            tops = []
            for c, line in enumerate(lines):
                s = mm_t(line[:, :HD], rows_qg[0, lanes, :]) * (SCALE * LOG2E)
                for b in range(size // BLOCK):
                    kb = c * (size // BLOCK) + b
                    part = s[b * BLOCK : (b + 1) * BLOCK]
                    if dy == 0 and half == 0 and kb < 2:
                        key = lax.broadcasted_iota(jnp.int32, (BLOCK, ROWS), 0)
                        row = lax.rem(lax.broadcasted_iota(jnp.int32, (BLOCK, ROWS), 1), BLOCK)
                        cut = [part[:, :ROWS], part[:, ROWS:]]
                        cut[kb] = jnp.where(key <= row, cut[kb], NEG)
                        part = jnp.concatenate(cut, axis=1)
                    p_all[kb * BLOCK : (kb + 1) * BLOCK, lanes] = part
                    tops.append(jnp.max(part.reshape(8, 8, LANES), axis=0) - biases[kb])
            while len(tops) > 1:
                tops = [jnp.maximum(tops[i], tops[i + 1]) for i in range(0, len(tops), 2)]
            top = jnp.max(tops[0], axis=0, keepdims=True)
            total, delta = jnp.zeros((8, LANES), F32), jnp.zeros((8, LANES), F32)
            for c, line in enumerate(lines):
                dp = mm_t(line[:, HD:], rows_qg[1, lanes, :])
                for b in range(size // BLOCK):
                    kb = c * (size // BLOCK) + b
                    rows = slice(kb * BLOCK, (kb + 1) * BLOCK)
                    dp_part = dp[b * BLOCK : (b + 1) * BLOCK]
                    p = jnp.exp2(p_all[rows, lanes] - (top + 3.0 * biases[kb]))
                    p_all[rows, lanes] = p
                    dp_all[rows, lanes] = dp_part
                    total += jnp.sum(p.reshape(8, 8, LANES), axis=0)
                    delta += jnp.sum((p * dp_part).reshape(8, 8, LANES), axis=0)
            total = jnp.sum(total, axis=0, keepdims=True)
            delta = jnp.sum(delta, axis=0, keepdims=True)
            stats[3:4, lanes] = top
            now = (top, total, delta)
            if before is not None:
                now = merge(stats_of(before, lanes), now)
            for k in range(3):
                stats[k : k + 1, lanes] = now[k]

    table = ("v", (LINE, ALL_ROWS), F32)
    args = (meta, rows_qg, *lines) + (() if before is None else (before,))
    pairs = LINE * ALL_ROWS
    return call(
        kernel, "stats", "s" + "v" * (len(args) - 1), [("v", (8, ALL_ROWS), F32), table, table], [],
        4 * pairs * HD, pairs, args,
    )


def swapped(came):
    halves = [stats_of(came, slice(h * LANES, (h + 1) * LANES)) for h in (1, 0)]
    return tuple(jnp.concatenate(pair, axis=1) for pair in zip(*halves))


def weights(own, final, came):
    top, total, delta = merge(stats_of(final), swapped(came))
    inv = 1.0 / total
    return jnp.exp2(own[3:4, :] - top) * inv, delta * inv


def grads_piece(rows_qg, piece, final, came, pieces, dtype):
    size = LINE // pieces

    def kernel(rows_qg, own, p_all, dp_all, final, came, *outs):
        w, delta = weights(own, final, came)
        step = 256
        for i in range(LINE // step):
            rows = slice(i * step, (i + 1) * step)
            p = p_all[rows, :] * w
            ds = (p * (dp_all[rows, :] - delta) * SCALE).astype(BF16)
            at = i * step // size
            dst = slice(i * step - at * size, (i + 1) * step - at * size)
            outs[at][dst, HD:] = mm(p.astype(BF16), rows_qg[1]).astype(dtype)
            outs[at][dst, :HD] = mm(ds, rows_qg[0]).astype(dtype)

    outs = [("v", (size, 2 * HD), dtype)] * pieces
    return call(
        kernel, "grads", "v" * 6, outs, [], 4 * LINE * ALL_ROWS * HD, 0, (rows_qg, *piece, final, came)
    )


def add_far(a, b, to_a, to_b):
    half = LINE // 2

    def kernel(a, b, to_a, to_b, out_a, out_b):
        out_a[:half] = a[:half].astype(BF16)
        out_a[half:] = (a[half:] + to_a[...].astype(F32)).astype(BF16)
        out_b[:half] = (b[:half] + to_b[...].astype(F32)).astype(BF16)
        out_b[half:] = b[half:].astype(BF16)

    line = ("v", (LINE, 2 * HD), BF16)
    return call(kernel, "add_far", "v" * 4, [line, line], [], 0, 0, (a, b, to_a, to_b))


def add_near(own, a, b):
    def kernel(own, a, b, *outs):
        for i, out in enumerate(outs):
            rows = slice(i * TOK, (i + 1) * TOK)
            out[...] = (own[rows, :] + a[rows, :].astype(F32) + b[rows, :].astype(F32)).astype(BF16)

    return call(kernel, "add_near", "v" * 3, [("v", (TOK, 2 * HD), BF16)] * 4, [], 0, 0, (own, a, b))


def query_grads(lines, pieces, final, came):
    counts = [len(group) for group in lines]

    def kernel(final, came, *refs):
        dq_own, dq_other, kt, dqt = refs[-4:]
        refs = list(refs[:-4])
        groups = [[refs.pop(0) for _ in range(n)] for n in counts]
        tables = [[refs.pop(0) for _ in range(3)] for _ in counts]
        for j, group in enumerate(groups):
            size = LINE // len(group)
            for c, line in enumerate(group):
                kt[j, :, c * size : (c + 1) * size] = line[:, :HD].T
        for half in range(ALL_ROWS // LANES):
            lanes = slice(half * LANES, (half + 1) * LANES)
            theirs = slice((1 - half) * LANES, (2 - half) * LANES)
            top, total, delta = merge(stats_of(final, lanes), stats_of(came, theirs))
            inv = 1.0 / total
            delta = delta * inv
            for j, (own, p_all, dp_all) in enumerate(tables):
                w = jnp.exp2(own[3:4, lanes] - top) * inv
                ds = (p_all[:, lanes] * w * (dp_all[:, lanes] - delta) * SCALE).astype(BF16)
                part = mm(kt[j], ds)
                dqt[...] = part if j == 0 else dqt[...] + part
            out = dqt[...].T
            for u in range(2):
                for h in range(QGROUP):
                    part = (slice(u * BLOCK, (u + 1) * BLOCK), slice(h * HD, (h + 1) * HD))
                    rows = slice(u * ROWS + h * BLOCK, u * ROWS + (h + 1) * BLOCK)
                    (dq_own, dq_other)[half][part] = out[rows, :]

    args = (final, came) + tuple(x for group in lines for x in group) + tuple(x for piece in pieces for x in piece)
    out = ("v", (TOK, QGROUP * HD), F32)
    scratch = [("v", (4, HD, LINE), BF16), ("v", (HD, LANES), F32)]
    return call(
        kernel, "queries", "v" * len(args), [out, out], scratch, 8 * LINE * ALL_ROWS * HD, 0, args
    )


def shards(queries, keys, values, out_grad, block_order):
    def swap(x):
        return lax.ppermute(x, "core", [(0, 1), (1, 0)])

    def shift(x, axis, s):
        return lax.ppermute(x, axis, [(i, (i + s) % 4) for i in range(4)])

    low = jnp.asarray(-jnp.inf, BF16)
    kv = jnp.maximum(lax.pad(keys, low, ((0, 0, 0), (0, HD, 0))), lax.pad(values, low, ((0, 0, 0), (HD, 0, 0))))
    line = join((kv, shift(kv, "x", 1), shift(kv, "x", 2), shift(kv, "x", 3)))
    up, down = shift(line, "y", 1), shift(line, "y", 3)
    far = (shift(down[: LINE // 2], "y", 3), shift(up[LINE // 2 :], "y", 1))
    place = lax.axis_index(("y", "x", "core")).astype(jnp.int32).reshape(1)
    meta, rows_qg = prepare(block_order, place, queries, swap(queries), out_grad, swap(out_grad))
    lines = ((line,), (up,), (down,), far)
    pieces, before = [], None
    for dy, group in zip((0, 1, 3, 2), lines):
        pieces.append(stats_piece(dy, meta, rows_qg, group, before))
        before = pieces[-1][0]
    came = swap(before)
    far1, far2 = grads_piece(rows_qg, pieces[3], before, came, 2, BF16)
    (up_part,) = grads_piece(rows_qg, pieces[1], before, came, 1, F32)
    (down_part,) = grads_piece(rows_qg, pieces[2], before, came, 1, F32)
    up_sum, down_sum = add_far(up_part, down_part, shift(far2, "y", 3), shift(far1, "y", 1))
    (own_part,) = grads_piece(rows_qg, pieces[0], before, came, 1, F32)
    parts = add_near(own_part, shift(up_sum, "y", 3), shift(down_sum, "y", 1))
    dq_own, dq_other = query_grads(lines, pieces, before, came)
    dq = (dq_own + swap(dq_other)).astype(BF16)
    dkv = parts[0].astype(F32)
    for s in (1, 2, 3):
        dkv = dkv + shift(parts[s], "x", 4 - s).astype(F32)
    mine = jnp.concatenate([dq, dkv.astype(BF16)], axis=1).reshape(8, TOK // 8, 10 * HD)
    got = lax.all_to_all(mine, "head", 0, 0, tiled=True).transpose(1, 0, 2)
    cols = [got[:, :, : 8 * HD], got[:, :, 8 * HD : 9 * HD], got[:, :, 9 * HD :]]
    return jnp.concatenate([c.reshape(TOK // 8, -1) for c in cols], axis=1)


def solution(mesh):
    split = Mesh(mesh.devices.reshape(4, 4, 2, 8), ("y", "x", "core", "head"))
    ctx = ("y", "x", "core")
    rows = P(ctx, "head")
    return jax.shard_map(
        shards,
        mesh=split,
        in_specs=(rows, rows, rows, rows, P()),
        out_specs=P(ctx + ("head",), None),
        check_vma=False,
    )
```
